256 devices in a mesh: leaf: 256 (over z, x, y, core).
Axes of the slice: x: 4, y: 4, z: 8, core: 2. Of those that a mesh axis runs over, the one named last changes fastest.
Arguments:
- points: bfloat16 [64, 524288], P(None, 'leaf'), may hold values from -6 to 6
- charges: bfloat16 [32, 524288], P(None, 'leaf'), may hold values from -0.59765625 to 0.59765625
- leaf_skel: int32 [256, 256], P('leaf'), may hold values from 0 to 2047, as said below
- up_skel: int32 [4, 256, 256], P(None, 'leaf'), may hold values from 0 to 511, as said below
- near_mask: int32 [256, 4], P('leaf'), may hold values from 0 to 1, as said below
Outputs:
- field: bfloat16 [32, 524288], P(None, 'leaf')
The draws below stay inside these ranges and needn't reach their ends.
Inputs may be any that keep to these rules, and one draw needn't show every extreme that they name: `leaf_skel`: each row holds 256 distinct positions. Each row holds 256 distinct positions; rows of the leaves under one node of level l+1 are equal in up_skel[l]. symmetric: near_mask[i, o] equals near_mask[i+o, -o]; zero where i + o falls outside the leaves.
All inputs are finite; a program needn't handle non-finite values.
Results may differ from the reference program's by a relative error of at most 0.0055.
Values may be sent and summed in bfloat16 or wider, within the bound.
No kernel may reach another device: no remote copies, remote signals or barrier semaphores. Data moves between devices by JAX's collectives and lax.ppermute only.
A program may use at most 64 MiB of HBM per device.

```python
import jax
import jax.numpy as jnp
from jax import lax

DIM = 64
LEAF_PTS = 2048
R = 256
RHS = 32
LEVELS = 4
TOTAL = 524288
NTOP = 16
N_LEAF = 256


def draw_points(key, part):
    key = jax.random.fold_in(key, 14)
    labels = jax.random.randint(jax.random.fold_in(key, 1), (TOTAL,), 0, 8)
    corner_bits = jax.random.randint(jax.random.fold_in(key, 2), (8, DIM), 0, 2)
    corner_signs = (2 * corner_bits - 1).astype(jnp.float32)
    placed = jnp.take(corner_signs, labels, axis=0).T
    amplitude = 1.5
    jitter = jax.random.normal(jax.random.fold_in(key, 3), (DIM, TOTAL), jnp.float32)
    return jnp.clip(amplitude * placed + jitter, -6.0, 6.0).astype(jnp.bfloat16)


def draw_leaf_skel(key, part):
    key = jax.random.fold_in(key, 11)
    keys = jax.random.split(key, N_LEAF)
    rows = jax.vmap(lambda sub: jax.random.permutation(sub, LEAF_PTS)[:R])(keys)
    return rows.astype(jnp.int32)


def draw_up_skel(key, part):
    key = jax.random.fold_in(key, 12)
    stacked = []
    for level in range(1, LEVELS + 1):
        nodes = N_LEAF // 2 ** level
        keys = jax.random.split(jax.random.fold_in(key, level), nodes)
        rows = jax.vmap(lambda sub: jax.random.permutation(sub, 2 * R)[:R])(keys)
        stacked.append(jnp.repeat(rows, 2 ** level, axis=0))
    return jnp.stack(stacked).astype(jnp.int32)


def draw_near_mask(key, part):
    key = jax.random.fold_in(key, 13)
    single = jax.random.randint(jax.random.fold_in(key, 1), (N_LEAF,), 0, 2)
    double = jax.random.randint(jax.random.fold_in(key, 2), (N_LEAF,), 0, 2)
    position = jnp.arange(N_LEAF)
    single = jnp.where(position < N_LEAF - 1, single, 0)
    double = jnp.where(position < N_LEAF - 2, double, 0)
    back_two = jnp.concatenate([jnp.zeros((2,), single.dtype), double[:-2]])
    back_one = jnp.concatenate([jnp.zeros((1,), single.dtype), single[:-1]])
    return jnp.stack([back_two, back_one, single, double], axis=1).astype(jnp.int32)


def level_of(rng, shape, cuts, low, largest):
    def one(dim, parts):
        steps = jax.random.uniform(jax.random.fold_in(jax.random.fold_in(rng, 6), dim), (parts,), jnp.float32, low / len(cuts), largest / len(cuts))
        return jnp.repeat(jnp.exp(steps), shape[dim] // parts).reshape((-1,) + (1,) * (len(shape) - dim - 1))

    loudness = one(*cuts[0])
    for cut in cuts[1:]:
        loudness = loudness * one(*cut)
    return loudness


def normal_values(own_key, dims, spread, most, pieces=(), kind=jnp.bfloat16):
    level = level_of(own_key, dims, pieces, -0.22, 0.18) if pieces else 1.0
    drawn = jax.random.normal(own_key, dims, jnp.float32) * spread * level
    return jnp.minimum(jnp.maximum(drawn, -most), most).astype(kind)


def setup_inputs(seed: int = 0) -> dict:
    streams_of = jax.random.split(jax.random.key(seed), 6)
    points = draw_points(jax.random.fold_in(streams_of[5], 71), 0)
    charges = normal_values(streams_of[1], (RHS, TOTAL), 0.1, 0.59765625, ((1, 256),))
    leaf_skel = draw_leaf_skel(jax.random.fold_in(streams_of[5], 71), 0)
    up_skel = draw_up_skel(jax.random.fold_in(streams_of[5], 71), 0)
    near_mask = draw_near_mask(jax.random.fold_in(streams_of[5], 71), 0)
    return dict(points=points, charges=charges, leaf_skel=leaf_skel, up_skel=up_skel, near_mask=near_mask)


def sq_dist(left, right):
    left_f = left.astype(jnp.float32)
    right_f = right.astype(jnp.float32)
    cross = lax.dot_general(left, right, (((0,), (0,)), ((), ())), preferred_element_type=jnp.float32)
    return jnp.sum(left_f * left_f, 0)[:, None] + jnp.sum(right_f * right_f, 0)[None, :] - 2.0 * cross


def kernel_tile(left, right):
    return jnp.exp(-sq_dist(left, right) / left.shape[0]).astype(jnp.bfloat16)


def interp(cands, chosen):
    weight = 1.0 / (1.0 + sq_dist(cands, chosen) / cands.shape[0])
    return (weight / jnp.sum(weight, 1, keepdims=True)).astype(jnp.bfloat16)


def reference(points, charges, leaf_skel, up_skel, near_mask):
    leaf_pts = points.reshape(DIM, N_LEAF, LEAF_PTS).transpose(1, 0, 2)
    leaf_chg = charges.reshape(RHS, N_LEAF, LEAF_PTS).transpose(1, 0, 2)
    leaf_ids = jnp.arange(N_LEAF, dtype=jnp.int32)
    shifts = (-2, -1, 1, 2)

    def near_leaf(leaf):
        own_pts = leaf_pts[leaf]
        total = jnp.dot(leaf_chg[leaf], kernel_tile(own_pts, own_pts), preferred_element_type=jnp.float32)
        for slot in range(4):
            other = jnp.clip(leaf + shifts[slot], 0, N_LEAF - 1).astype(jnp.int32)
            term = lax.cond(near_mask[leaf, slot] > 0,
                            lambda idx: jnp.dot(leaf_chg[idx], kernel_tile(leaf_pts[idx], own_pts), preferred_element_type=jnp.float32),
                            lambda idx: jnp.zeros((RHS, LEAF_PTS), jnp.float32), other)
            total = total + term
        return total

    skeleton = jax.vmap(lambda block, picks: jnp.take(block, picks, axis=1))(leaf_pts, leaf_skel)

    def leaf_charge(leaf):
        weights = interp(leaf_pts[leaf], skeleton[leaf])
        return jnp.dot(leaf_chg[leaf], weights, preferred_element_type=jnp.float32).astype(jnp.bfloat16)

    node_chg = lax.map(leaf_charge, leaf_ids)
    node_pts = skeleton
    couplings = []
    transfers = []

    def couple(target, source, source_chg):
        return jnp.dot(source_chg, kernel_tile(source, target), preferred_element_type=jnp.float32)

    for level in range(1, LEVELS + 1):
        count = node_pts.shape[0] // 2
        pair_pts = node_pts.reshape(count, 2, DIM, R)
        pair_chg = node_chg.reshape(count, 2, RHS, R)
        lower_p, upper_p = pair_pts[:, 0], pair_pts[:, 1]
        lower_c, upper_c = pair_chg[:, 0], pair_chg[:, 1]
        to_lower = jax.vmap(couple)(lower_p, upper_p, upper_c)
        to_upper = jax.vmap(couple)(upper_p, lower_p, lower_c)
        couplings.append(jnp.stack([to_lower, to_upper], 1).reshape(count * 2, RHS, R))
        joined_pts = jnp.concatenate([lower_p, upper_p], axis=2)
        joined_chg = jnp.concatenate([lower_c, upper_c], axis=2)
        picks = up_skel[level - 1, ::2 ** level]
        parent_pts = jax.vmap(lambda block, chosen: jnp.take(block, chosen, axis=1))(joined_pts, picks)
        transfer = jax.vmap(interp)(joined_pts, parent_pts)
        parent_chg = jax.vmap(lambda block, mat: jnp.dot(block, mat, preferred_element_type=jnp.float32))(joined_chg, transfer).astype(jnp.bfloat16)
        transfers.append(transfer)
        node_pts, node_chg = parent_pts, parent_chg

    all_pts = node_pts.transpose(1, 0, 2).reshape(DIM, NTOP * R)
    all_chg = node_chg.transpose(1, 0, 2).reshape(RHS, NTOP * R)
    owner = jnp.arange(NTOP * R, dtype=jnp.int32) // R

    def top_far(node):
        masked = jnp.where(owner[None, :] == node, jnp.zeros((), jnp.bfloat16), all_chg)
        return jnp.dot(masked, kernel_tile(all_pts, node_pts[node]), preferred_element_type=jnp.float32)

    potential = lax.map(top_far, jnp.arange(NTOP, dtype=jnp.int32))

    def descend(halves, upper):
        return jax.vmap(lambda half: lax.dot_general(upper, half, (((1,), (1,)), ((), ())), preferred_element_type=jnp.float32))(halves)

    for level in range(LEVELS, 0, -1):
        transfer = transfers[level - 1]
        count = transfer.shape[0]
        halves = transfer.reshape(count, 2, R, R)
        child = jax.vmap(descend)(halves, potential.astype(jnp.bfloat16))
        potential = child.reshape(count * 2, RHS, R) + couplings[level - 1]

    def leaf_out(leaf):
        weights = interp(leaf_pts[leaf], skeleton[leaf])
        far_part = lax.dot_general(potential[leaf].astype(jnp.bfloat16), weights, (((1,), (1,)), ((), ())), preferred_element_type=jnp.float32)
        return (near_leaf(leaf) + far_part).astype(jnp.bfloat16)

    result = lax.map(leaf_out, leaf_ids)
    return result.transpose(1, 0, 2).reshape(RHS, TOTAL)
```

```python
import functools

import jax
import jax.numpy as jnp
from jax import lax
import jax.experimental.pallas as pl
import jax.experimental.pallas.tpu as pltpu
from jax.sharding import PartitionSpec as P

f32 = jnp.float32
bf16 = jnp.bfloat16
LOG2E = 1.4426950408889634
DIM = 64
AUG = 80
VMEM_LIMIT = 40 * 2**20


def params():
    return pltpu.CompilerParams(vmem_limit_bytes=VMEM_LIMIT)


VM = pl.BlockSpec(memory_space=pltpu.VMEM)
SM = pl.BlockSpec(memory_space=pltpu.SMEM)
ANY = pl.BlockSpec(memory_space=pl.ANY)


def norm_parts(pts):
    wide = pts.astype(f32)
    norm = jnp.sum(wide * wide, axis=0, keepdims=True)
    high = norm.astype(bf16).astype(f32)
    rest = norm - high
    mid = rest.astype(bf16).astype(f32)
    return high, mid, rest - mid


def extra_rows(first, second, count):
    row = lax.broadcasted_iota(jnp.int32, (16, count), 0)
    out = jnp.zeros((16, count), f32)
    for place, value in enumerate(tuple(first) + tuple(second)):
        out = jnp.where(row == place, value, out)
    return out.astype(bf16)


def source_form(pts):
    ones = (1.0, 1.0, 1.0)
    return jnp.concatenate([pts, extra_rows(norm_parts(pts), ones, pts.shape[1])], axis=0)


def target_form(pts):
    inv = 1.0 / DIM
    parts = norm_parts(pts)
    scaled = (pts.astype(f32) * (2.0 * inv)).astype(bf16)
    return jnp.concatenate(
        [scaled, extra_rows((-inv, -inv, -inv), [-inv * p for p in parts], pts.shape[1])], axis=0
    )


def contract_rows(left, right):
    return lax.dot_general(left, right, (((0,), (0,)), ((), ())), preferred_element_type=f32)


def contract_cols(left, right):
    return lax.dot_general(left, right, (((1,), (1,)), ((), ())), preferred_element_type=f32)


def gauss(neg_dist):
    return jnp.exp2(neg_dist * LOG2E).astype(bf16)


def interp_t(neg_dist):
    weight = 1.0 / (1.0 - neg_dist)
    total = jnp.sum(weight, axis=0, keepdims=True)
    return (weight * (1.0 / total)).astype(bf16)


def prep_kernel(points, charges, skel, block, target_t, chosen):
    pts = points[...]
    block[:AUG, :] = source_form(pts)
    block[AUG:, :] = charges[...]
    tgt = target_form(pts)
    count = pts.shape[1]
    pad = jnp.zeros((128 - AUG, 256), f32)
    for start in range(0, count, 256):
        piece = jnp.concatenate([tgt[:, start : start + 256].astype(f32), pad], axis=0)
        target_t[start : start + 256, :] = piece.T.astype(bf16)
    rank = skel.shape[1]
    spots = lax.broadcasted_iota(jnp.int32, (count, rank), 0)
    pick = jnp.where(spots == skel[...], 1.0, 0.0).astype(bf16)
    chosen[...] = jnp.dot(pts, pick, preferred_element_type=f32).astype(bf16)


def prep(points, charges, skel):
    count = points.shape[1]
    return pl.pallas_call(
        prep_kernel,
        out_shape=(
            jax.ShapeDtypeStruct((AUG + charges.shape[0], count), bf16),
            jax.ShapeDtypeStruct((count, 128), bf16),
            jax.ShapeDtypeStruct((DIM, skel.shape[1]), bf16),
        ),
        in_specs=[VM, VM, VM],
        out_specs=(VM, VM, VM),
        compiler_params=params(),
        name="prep",
    )(points, charges, skel)


def leaf_kernel(block, chosen, weights_t, node):
    chosen_pts = chosen[...]
    tgt = target_form(chosen_pts)
    weights = interp_t(contract_rows(tgt, block[:AUG, :]))
    weights_t[...] = weights
    node[:DIM, :] = chosen_pts
    node[DIM:, :] = contract_cols(block[AUG:, :], weights).astype(bf16)


def leaf(block, chosen):
    rank = chosen.shape[1]
    count = block.shape[1]
    rows = DIM + block.shape[0] - AUG
    return pl.pallas_call(
        leaf_kernel,
        out_shape=(
            jax.ShapeDtypeStruct((rank, count), bf16),
            jax.ShapeDtypeStruct((rows, rank), bf16),
        ),
        in_specs=[VM, VM],
        out_specs=(VM, VM),
        compiler_params=params(),
        name="leaf",
    )(block, chosen)


def near_kernel(slots, mask, block, target_t, before, token, total):
    odd = lax.axis_index("leaf") % 2
    if slots is None:
        wanted = None
    else:
        wanted = jnp.where(odd == 1, mask[0, slots[1]], mask[0, slots[0]]) > 0
    count = target_t.shape[0]
    step = 256
    piece = 512

    def tile():
        for start in range(0, count, step):
            acc = None
            for src in range(0, count, piece):
                neg = jnp.dot(
                    target_t[start : start + step, :AUG],
                    block[:AUG, src : src + piece],
                    preferred_element_type=f32,
                )
                part = contract_cols(gauss(neg), block[AUG:, src : src + piece])
                acc = part if acc is None else acc + part
            if slots is None:
                total[:, start : start + step] = acc.T
            else:
                total[:, start : start + step] = before[:, start : start + step] + acc.T

    if slots is None:
        tile()
    else:
        pl.when(wanted)(tile)

        @pl.when(jnp.logical_not(wanted))
        def _():
            total[...] = before[...]


def near(slots, mask, block, target_t, before, token):
    count = target_t.shape[0]
    rows = block.shape[0] - AUG
    return pl.pallas_call(
        functools.partial(near_kernel, slots),
        out_shape=jax.ShapeDtypeStruct((rows, count), f32),
        in_specs=[SM, VM, VM, VM if slots is not None else ANY, ANY],
        out_specs=VM,
        compiler_params=params(),
        cost_estimate=pl.CostEstimate(flops=4 * 10**9, bytes_accessed=10**6, transcendentals=0),
        name="near",
    )(mask, block, target_t, before, token)


def level_kernel(level, up, node, partner, token, coupling, half_t, parent):
    upper = (lax.axis_index("leaf") >> (level - 1)) & 1
    rank = node.shape[1]
    picks = up[level - 1]
    rows = lax.broadcasted_iota(jnp.int32, (rank, rank), 0)
    own_pick = jnp.where(rows + upper * rank == picks, 1.0, 0.0).astype(bf16)
    other_pick = jnp.where(rows + (1 - upper) * rank == picks, 1.0, 0.0).astype(bf16)
    own = node[:DIM, :]
    other = partner[:DIM, :]
    chosen = (
        jnp.dot(own, own_pick, preferred_element_type=f32)
        + jnp.dot(other, other_pick, preferred_element_type=f32)
    ).astype(bf16)
    own_tgt = target_form(own)
    chosen_tgt = target_form(chosen)
    other_src = source_form(other)
    own_src = source_form(own)
    own_half = interp_t(contract_rows(chosen_tgt, own_src))
    other_half = interp_t(contract_rows(chosen_tgt, other_src))
    half_t[...] = own_half
    charges = contract_cols(node[DIM:, :], own_half) + contract_cols(partner[DIM:, :], other_half)
    parent[:DIM, :] = chosen
    parent[DIM:, :] = charges.astype(bf16)
    kern = gauss(contract_rows(other_src, own_tgt))
    coupling[...] = jnp.dot(partner[DIM:, :], kern, preferred_element_type=f32)


def climb(level, up, node, partner, token):
    rows, rank = node.shape
    return pl.pallas_call(
        functools.partial(level_kernel, level),
        out_shape=(
            jax.ShapeDtypeStruct((rows - DIM, rank), f32),
            jax.ShapeDtypeStruct((rank, rank), bf16),
            jax.ShapeDtypeStruct((rows, rank), bf16),
        ),
        in_specs=[VM, VM, VM, ANY],
        out_specs=(VM, VM, VM),
        compiler_params=params(),
        name="climb",
    )(up, node, partner, token)


def top_kernel(levels, node, source, token, potential):
    group = 2**levels
    index = lax.axis_index("leaf")
    other = (index >> levels) != (index & (group - 1))
    kern = gauss(contract_rows(source_form(source[:DIM, :]), target_form(node[:DIM, :])))
    part = jnp.dot(source[DIM:, :], kern, preferred_element_type=f32)
    potential[...] = jnp.where(other, part, 0.0)


def top(levels, node, source, token):
    rows, rank = node.shape
    return pl.pallas_call(
        functools.partial(top_kernel, levels),
        out_shape=jax.ShapeDtypeStruct((rows - DIM, rank), f32),
        in_specs=[VM, VM, ANY],
        out_specs=VM,
        compiler_params=params(),
        name="top",
    )(node, source, token)


def down_kernel(levels, *refs):
    potential, last, total, weights_t = refs[:4]
    couplings = refs[4 : 4 + levels]
    halves = refs[4 + levels : 4 + 2 * levels]
    out = refs[-1]
    wave = potential[...] + last[...]
    for level in range(levels, 0, -1):
        wave = (
            jnp.dot(wave.astype(bf16), halves[level - 1][...], preferred_element_type=f32)
            + couplings[level - 1][...]
        )
    far = jnp.dot(wave.astype(bf16), weights_t[...], preferred_element_type=f32)
    out[...] = (total[...] + far).astype(bf16)


def down(potential, last, total, weights_t, couplings, halves):
    levels = len(couplings)
    return pl.pallas_call(
        functools.partial(down_kernel, levels),
        out_shape=jax.ShapeDtypeStruct(total.shape, bf16),
        in_specs=[VM] * (4 + 2 * levels),
        out_specs=VM,
        compiler_params=params(),
        name="down",
    )(potential, last, total, weights_t, *couplings, *halves)


def body(points, charges, leaf_skel, up_skel, near_mask):
    levels = up_skel.shape[0]
    group = 2**levels
    devices = lax.axis_size("leaf")

    def send(value, target):
        pairs = [(i, target(i)) for i in range(devices) if 0 <= target(i) < devices]
        return lax.ppermute(value, "leaf", pairs)

    block, target_t, chosen = prep(points, charges, leaf_skel)
    mate = send(block, lambda i: i ^ 1)
    across = send(block, lambda i: i + 1 if i % 2 else i - 1)
    second = send(block, lambda i: i - 2 if i % 2 else i + 2)
    weights_t, node = leaf(block, chosen)
    total = near(None, near_mask, block, target_t, node, node)
    couplings, halves = [], []
    token = node
    for level in range(1, levels + 1):
        partner = send(node, lambda i: i ^ 2 ** (level - 1))
        if level == 2:
            total = near((2, 1), near_mask, mate, target_t, total, node)
        if level == 3:
            passed = send(across, lambda i: i ^ 1)
        if level == 4:
            total = near((1, 2), near_mask, across, target_t, total, node)
        coupling, half_t, node = climb(level, up_skel, node, partner, total)
        couplings.append(coupling)
        halves.append(half_t)
    source = send(node, lambda i: (i % group) * group + i // group)
    total = near((0, 3), near_mask, second, target_t, total, node)
    wave = top(levels, node, source, total)
    for step in range(levels):
        arrived = send(wave, lambda i: i ^ 2**step)
        if step == 1:
            total = near((3, 0), near_mask, passed, target_t, total, wave)
        if step < levels - 1:
            wave = wave + arrived
    return down(wave, arrived, total, weights_t, couplings, halves)


def solution(mesh):
    return jax.shard_map(
        body,
        mesh=mesh,
        in_specs=(
            P(None, "leaf"),
            P(None, "leaf"),
            P("leaf", None),
            P(None, "leaf", None),
            P("leaf", None),
        ),
        out_specs=P(None, "leaf"),
        check_vma=False,
    )
```

```python
import functools

import jax
import jax.numpy as jnp
from jax import lax
import jax.experimental.pallas as pl
import jax.experimental.pallas.tpu as pltpu
from jax.sharding import PartitionSpec as P

f32 = jnp.float32
bf16 = jnp.bfloat16
LOG2E = 1.4426950408889634
DIM = 64
STEP = 256
PIECE = 1024
AUG = 80


def params(mib=24):
    return pltpu.CompilerParams(vmem_limit_bytes=mib * 2**20)


VM = pl.BlockSpec(memory_space=pltpu.VMEM)
SM = pl.BlockSpec(memory_space=pltpu.SMEM)
ANY = pl.BlockSpec(memory_space=pl.ANY)
HBM = pl.BlockSpec(memory_space=pltpu.HBM)


def norm_parts(pts):
    wide = pts.astype(f32)
    norm = jnp.sum(wide * wide, axis=0, keepdims=True)
    high = norm.astype(bf16).astype(f32)
    rest = norm - high
    mid = rest.astype(bf16).astype(f32)
    return high, mid, rest - mid


def extra_rows(first, second, count):
    row = lax.broadcasted_iota(jnp.int32, (16, count), 0)
    out = jnp.zeros((16, count), f32)
    for place, value in enumerate(tuple(first) + tuple(second)):
        out = jnp.where(row == place, value, out)
    return out.astype(bf16)


def source_form(pts):
    ones = (1.0, 1.0, 1.0)
    return jnp.concatenate([pts, extra_rows(norm_parts(pts), ones, pts.shape[1])], axis=0)


def target_form(pts):
    inv = 1.0 / DIM
    parts = norm_parts(pts)
    scaled = (pts.astype(f32) * (2.0 * inv)).astype(bf16)
    return jnp.concatenate(
        [scaled, extra_rows((-inv, -inv, -inv), [-inv * p for p in parts], pts.shape[1])], axis=0
    )


def contract_rows(left, right):
    return lax.dot_general(left, right, (((0,), (0,)), ((), ())), preferred_element_type=f32)


def contract_cols(left, right):
    return lax.dot_general(left, right, (((1,), (1,)), ((), ())), preferred_element_type=f32)


def gauss(neg_dist):
    return jnp.exp2(neg_dist * LOG2E).astype(bf16)


def interp_t(neg_dist):
    weight = 1.0 / (1.0 - neg_dist)
    total = jnp.sum(weight, axis=0, keepdims=True)
    return (weight * (1.0 / total)).astype(bf16)


def leaf_kernel(points, charges, skel, weights_t, node, block, skel_v, sems):
    copies = [
        pltpu.make_async_copy(points, block.at[:DIM], sems.at[0]),
        pltpu.make_async_copy(skel, skel_v, sems.at[1]),
        pltpu.make_async_copy(charges, block.at[DIM:], sems.at[2]),
    ]
    for copy in copies:
        copy.start()
    copies[0].wait()
    copies[1].wait()
    pts = block[:DIM, :]
    rank = skel_v.shape[1]
    spots = lax.broadcasted_iota(jnp.int32, (pts.shape[1], rank), 0)
    pick = jnp.where(spots == skel_v[...], 1.0, 0.0).astype(bf16)
    chosen = jnp.dot(pts, pick, preferred_element_type=f32).astype(bf16)
    weights = interp_t(contract_rows(target_form(chosen), source_form(pts)))
    weights_t[...] = weights
    node[:DIM, :] = chosen
    copies[2].wait()
    node[DIM:, :] = contract_cols(block[DIM:, :], weights).astype(bf16)


def leaf(points, charges, skel):
    rank = skel.shape[1]
    count = points.shape[1]
    rows = DIM + charges.shape[0]
    return pl.pallas_call(
        leaf_kernel,
        out_shape=(
            jax.ShapeDtypeStruct((rank, count), bf16),
            jax.ShapeDtypeStruct((rows, rank), bf16),
            jax.ShapeDtypeStruct((rows, count), bf16),
        ),
        in_specs=[HBM, HBM, HBM],
        out_specs=(VM, VM, VM),
        scratch_shapes=[pltpu.VMEM(skel.shape, jnp.int32), pltpu.SemaphoreType.DMA((3,))],
        compiler_params=params(),
        name="leaf",
    )(points, charges, skel)


def transposed(form):
    count = form.shape[1]
    pad = jnp.zeros((128 - AUG, count), f32)
    return jnp.concatenate([form.astype(f32), pad], axis=0).T.astype(bf16)


def prep_kernel(block, token, source, target):
    pts = block[:DIM, :]
    source[...] = transposed(source_form(pts))
    target[...] = target_form(pts)


def prep(block, token):
    count = block.shape[1]
    return pl.pallas_call(
        prep_kernel,
        out_shape=(
            jax.ShapeDtypeStruct((count, 128), bf16),
            jax.ShapeDtypeStruct((AUG, count), bf16),
        ),
        in_specs=[VM, ANY],
        out_specs=(VM, VM),
        compiler_params=params(),
        name="prep",
    )(block, token)


def near_columns(source, charges, target, out, first, width):
    count = source.shape[0]
    waiting = ready = None
    sums = {}

    def finish(col, src, kern):
        part = jnp.dot(charges[DIM:, src : src + PIECE], kern, preferred_element_type=f32)
        sums[col] = part if src == 0 else sums[col] + part
        if src + PIECE == count:
            out[:, col : col + STEP] = sums.pop(col)

    for col in range(0, width, STEP):
        for src in range(0, count, PIECE):
            inner = jnp.dot(
                source[src : src + PIECE, :AUG],
                target[:, first + col : first + col + STEP],
                preferred_element_type=f32,
            )
            if ready is not None:
                finish(*ready)
                ready = None
            if waiting is not None:
                ready = (waiting[0], waiting[1], gauss(waiting[2]))
            waiting = (col, src, inner)
    if ready is not None:
        finish(*ready)
    finish(waiting[0], waiting[1], gauss(waiting[2]))


def near_kernel(slots, width, fresh, mask, block, *refs):
    if fresh:
        target, _, out, source = refs
    else:
        source, target, _, out = refs

    def tile():
        if fresh:
            source[...] = transposed(source_form(block[:DIM, :]))
        near_columns(source, block, target, out, width[0], width[1])

    if slots is None:
        tile()
        return
    odd = lax.axis_index("leaf") % 2
    wanted = jnp.where(odd == 1, mask[0, slots[1]], mask[0, slots[0]]) > 0
    pl.when(wanted)(tile)

    @pl.when(jnp.logical_not(wanted))
    def _():
        out[...] = jnp.zeros_like(out)


def near(slots, first, width, mask, block, source, target, token):
    fresh = source is None
    rows = block.shape[0] - DIM
    count = target.shape[1]
    arrays = (mask, block) + (() if fresh else (source,)) + (target, token)
    return pl.pallas_call(
        functools.partial(near_kernel, slots, (first, width), fresh),
        out_shape=jax.ShapeDtypeStruct((rows, width), f32),
        in_specs=[SM] + [VM] * (len(arrays) - 2) + [ANY],
        out_specs=VM,
        scratch_shapes=[pltpu.VMEM((count, 128), bf16)] if fresh else [],
        compiler_params=params(),
        cost_estimate=pl.CostEstimate(flops=4 * 10**9 * width // count, bytes_accessed=10**6, transcendentals=0),
        name="near",
    )(*arrays)


def level_kernel(level, up, node, partner, token, half_t, parent):
    upper = (lax.axis_index("leaf") >> (level - 1)) & 1
    rank = node.shape[1]
    picks = up[level - 1]
    rows = lax.broadcasted_iota(jnp.int32, (rank, rank), 0)
    own_pick = jnp.where(rows + upper * rank == picks, 1.0, 0.0).astype(bf16)
    other_pick = jnp.where(rows + (1 - upper) * rank == picks, 1.0, 0.0).astype(bf16)
    own = node[:DIM, :]
    other = partner[:DIM, :]
    chosen = (
        jnp.dot(own, own_pick, preferred_element_type=f32)
        + jnp.dot(other, other_pick, preferred_element_type=f32)
    ).astype(bf16)
    chosen_tgt = target_form(chosen)
    own_half = interp_t(contract_rows(chosen_tgt, source_form(own)))
    other_half = interp_t(contract_rows(chosen_tgt, source_form(other)))
    half_t[...] = own_half
    charges = contract_cols(node[DIM:, :], own_half) + contract_cols(partner[DIM:, :], other_half)
    parent[:DIM, :] = chosen
    parent[DIM:, :] = charges.astype(bf16)


def climb(level, up, node, partner, token):
    rows, rank = node.shape
    return pl.pallas_call(
        functools.partial(level_kernel, level),
        out_shape=(
            jax.ShapeDtypeStruct((rank, rank), bf16),
            jax.ShapeDtypeStruct((rows, rank), bf16),
        ),
        in_specs=[VM, VM, VM, ANY],
        out_specs=(VM, VM),
        compiler_params=params(),
        name="climb",
    )(up, node, partner, token)


def couple_kernel(levels, *refs):
    for level in range(levels):
        node, partner, out = refs[level], refs[levels + level], refs[2 * levels + 1 + level]
        kern = gauss(contract_rows(source_form(partner[:DIM, :]), target_form(node[:DIM, :])))
        out[...] = jnp.dot(partner[DIM:, :], kern, preferred_element_type=f32)


def couple(nodes, partners, token):
    levels = len(nodes)
    rows, rank = nodes[0].shape
    return pl.pallas_call(
        functools.partial(couple_kernel, levels),
        out_shape=(jax.ShapeDtypeStruct((rows - DIM, rank), f32),) * levels,
        in_specs=[VM] * (2 * levels) + [ANY],
        out_specs=(VM,) * levels,
        compiler_params=params(),
        name="couple",
    )(*nodes, *partners, token)


def top_kernel(levels, node, source, token, potential):
    place = lax.axis_index("leaf") & (2**levels - 1)
    kern = gauss(contract_rows(source_form(source[:DIM, :]), target_form(node[:DIM, :])))
    part = jnp.dot(source[DIM:, :], kern, preferred_element_type=f32)
    potential[...] = jnp.where(place != 0, part, 0.0)


def top(levels, node, source, token):
    rows, rank = node.shape
    return pl.pallas_call(
        functools.partial(top_kernel, levels),
        out_shape=jax.ShapeDtypeStruct((rows - DIM, rank), f32),
        in_specs=[VM, VM, ANY],
        out_specs=VM,
        compiler_params=params(),
        name="top",
    )(node, source, token)


def down_kernel(levels, starts, *refs):
    potential, last, weights_t = refs[:3]
    couplings = refs[3 : 3 + levels]
    halves = refs[3 + levels : 3 + 2 * levels]
    pieces = refs[3 + 2 * levels : -1]
    out = refs[-1]
    wave = potential[...] + last[...]
    for level in range(levels, 0, -1):
        wave = (
            jnp.dot(wave.astype(bf16), halves[level - 1][...], preferred_element_type=f32)
            + couplings[level - 1][...]
        )
    wave = wave.astype(bf16)
    for col in range(0, out.shape[1], STEP):
        total = None
        for start, piece in zip(starts, pieces):
            if start <= col < start + piece.shape[1]:
                part = piece[:, col - start : col - start + STEP]
                total = part if total is None else total + part
        far = jnp.dot(wave, weights_t[:, col : col + STEP], preferred_element_type=f32)
        out[:, col : col + STEP] = (total + far).astype(bf16)


def down(potential, last, weights_t, couplings, halves, pieces):
    levels = len(couplings)
    starts = [start for start, _ in pieces]
    arrays = (potential, last, weights_t, *couplings, *halves, *(p for _, p in pieces))
    return pl.pallas_call(
        functools.partial(down_kernel, levels, starts),
        out_shape=jax.ShapeDtypeStruct((potential.shape[0], weights_t.shape[1]), bf16),
        in_specs=[VM] * len(arrays),
        out_specs=VM,
        compiler_params=params(),
        name="down",
    )(*arrays)


def after(value, token):
    return lax.optimization_barrier((value, token))[0]


def body(points, charges, leaf_skel, up_skel, near_mask):
    levels = up_skel.shape[0]
    devices = lax.axis_size("leaf")
    pieces = []

    def send(value, target):
        pairs = [(i, target(i) % devices) for i in range(devices)]
        return lax.ppermute(value, "leaf", pairs)

    weights_t, node, block = leaf(points, charges, leaf_skel)
    nodes, partners, halves = [], [], []

    def exchange(mask):
        nodes.append(node)
        partners.append(send(node, lambda i: i ^ mask))

    def step(level, token):
        half_t, parent = climb(level, up_skel, nodes[-1], partners[-1], token)
        halves.append(half_t)
        return parent

    def piece(slots, first, width, block, source, token):
        out = near(slots, first, width, near_mask, block, source, target, token)
        pieces.append((first, out))
        return out

    exchange(1)
    mate = send(after(block, node), lambda i: i ^ 1)
    source, target = prep(block, node)
    node = step(1, target)
    exchange(2)
    across = send(after(block, node), lambda i: i + 1 if i % 2 else i - 1)
    token = piece(None, 0, 256, block, source, node)
    node = step(2, token)
    exchange(6)
    second = send(after(block, node), lambda i: i - 2 if i % 2 else i + 2)
    token = piece(None, 256, 256, block, source, node)
    node = step(3, token)
    exchange(8)
    token = piece(None, 512, 1536, block, source, node)
    node = step(4, token)
    couplings = couple(nodes, partners, node)
    arrived = send(node, lambda i: i ^ (((i & 7) << 5 | (i >> 3 & 1) << 4) or 16))
    passed = send(after(across, node), lambda i: i ^ 1)
    token = piece((2, 1), 0, 2048, mate, None, couplings[0])
    wave = top(levels, node, arrived, token)
    arrived = send(wave, lambda i: i ^ 1)
    wave = wave + arrived
    arrived = send(wave, lambda i: i ^ 2)
    token = piece((1, 2), 0, 2048, across, None, wave)
    wave = wave + after(arrived, token)
    arrived = send(wave, lambda i: i ^ 6)
    token = piece((0, 3), 0, 2048, second, None, wave)
    wave = wave + after(arrived, token)
    arrived = send(wave, lambda i: i ^ 8)
    token = piece((3, 0), 0, 2048, passed, None, wave)
    return down(wave, arrived, weights_t, couplings, halves, pieces)


def solution(mesh):
    return jax.shard_map(
        body,
        mesh=mesh,
        in_specs=(
            P(None, "leaf"),
            P(None, "leaf"),
            P("leaf", None),
            P(None, "leaf", None),
            P("leaf", None),
        ),
        out_specs=P(None, "leaf"),
        check_vma=False,
    )
```

```python
import functools

import jax
import jax.numpy as jnp
from jax import lax
import jax.experimental.pallas as pl
import jax.experimental.pallas.tpu as pltpu
from jax.sharding import PartitionSpec as P

f32 = jnp.float32
bf16 = jnp.bfloat16
LOG2E = 1.4426950408889634
DIM = 64
STEP = 256
PIECE = 1024
AUG = 80


def params(mib=24):
    return pltpu.CompilerParams(vmem_limit_bytes=mib * 2**20)


VM = pl.BlockSpec(memory_space=pltpu.VMEM)
SM = pl.BlockSpec(memory_space=pltpu.SMEM)
ANY = pl.BlockSpec(memory_space=pl.ANY)

SLOTS = ((2, 1), (1, 2), (0, 3), (3, 0))


def norm_parts(pts):
    wide = pts.astype(f32)
    norm = jnp.sum(wide * wide, axis=0, keepdims=True)
    high = norm.astype(bf16).astype(f32)
    rest = norm - high
    mid = rest.astype(bf16).astype(f32)
    return high, mid, rest - mid


def extra_rows(first, second, count):
    row = lax.broadcasted_iota(jnp.int32, (16, count), 0)
    out = jnp.zeros((16, count), f32)
    for place, value in enumerate(tuple(first) + tuple(second)):
        out = jnp.where(row == place, value, out)
    return out.astype(bf16)


def source_form(pts):
    ones = (1.0, 1.0, 1.0)
    return jnp.concatenate([pts, extra_rows(norm_parts(pts), ones, pts.shape[1])], axis=0)


def target_form(pts):
    inv = 1.0 / DIM
    parts = norm_parts(pts)
    scaled = (pts.astype(f32) * (2.0 * inv)).astype(bf16)
    return jnp.concatenate(
        [scaled, extra_rows((-inv, -inv, -inv), [-inv * p for p in parts], pts.shape[1])], axis=0
    )


def contract_rows(left, right):
    return lax.dot_general(left, right, (((0,), (0,)), ((), ())), preferred_element_type=f32)


def contract_cols(left, right):
    return lax.dot_general(left, right, (((1,), (1,)), ((), ())), preferred_element_type=f32)


def gauss(neg_dist):
    return jnp.exp2(neg_dist * LOG2E).astype(bf16)


def interp_t(neg_dist):
    weight = 1.0 / (1.0 - neg_dist)
    total = jnp.sum(weight, axis=0, keepdims=True)
    return (weight * (1.0 / total)).astype(bf16)


def first_kernel(out):
    out[...] = jnp.zeros_like(out)


def first():
    return pl.pallas_call(
        first_kernel,
        out_shape=jax.ShapeDtypeStruct((8, 128), f32),
        out_specs=VM,
        compiler_params=params(),
        cost_estimate=pl.CostEstimate(flops=4 * 10**9, bytes_accessed=10**6, transcendentals=0),
        name="first",
    )()


def leaf_kernel(points, charges, skel, token, weights_t, node, block):
    pts = points[...]
    block[:DIM, :] = pts
    block[DIM:, :] = charges[...]
    rank = skel.shape[1]
    spots = lax.broadcasted_iota(jnp.int32, (pts.shape[1], rank), 0)
    pick = jnp.where(spots == skel[...], 1.0, 0.0).astype(bf16)
    chosen = jnp.dot(pts, pick, preferred_element_type=f32).astype(bf16)
    weights = interp_t(contract_rows(target_form(chosen), source_form(pts)))
    weights_t[...] = weights
    node[:DIM, :] = chosen
    node[DIM:, :] = contract_cols(charges[...], weights).astype(bf16)


def leaf(points, charges, skel, token):
    rank = skel.shape[1]
    count = points.shape[1]
    rows = DIM + charges.shape[0]
    return pl.pallas_call(
        leaf_kernel,
        out_shape=(
            jax.ShapeDtypeStruct((rank, count), bf16),
            jax.ShapeDtypeStruct((rows, rank), bf16),
            jax.ShapeDtypeStruct((rows, count), bf16),
        ),
        in_specs=[VM, VM, VM, ANY],
        out_specs=(VM, VM, VM),
        compiler_params=params(),
        name="leaf",
    )(points, charges, skel, token)


def transposed(form):
    count = form.shape[1]
    pad = jnp.zeros((128 - AUG, count), f32)
    return jnp.concatenate([form.astype(f32), pad], axis=0).T.astype(bf16)


def prep_kernel(block, token, source, target):
    pts = block[:DIM, :]
    source[...] = transposed(source_form(pts))
    target[...] = target_form(pts)


def prep(block, token):
    count = block.shape[1]
    return pl.pallas_call(
        prep_kernel,
        out_shape=(
            jax.ShapeDtypeStruct((count, 128), bf16),
            jax.ShapeDtypeStruct((AUG, count), bf16),
        ),
        in_specs=[VM, ANY],
        out_specs=(VM, VM),
        compiler_params=params(),
        name="prep",
    )(block, token)


def near_columns(source, charges, target, out, first, width):
    count = source.shape[0]
    waiting = ready = None
    sums = {}

    def finish(col, src, kern):
        part = jnp.dot(charges[DIM:, src : src + PIECE], kern, preferred_element_type=f32)
        sums[col] = part if src == 0 else sums[col] + part
        if src + PIECE == count:
            out[:, col : col + STEP] = sums.pop(col)

    for col in range(0, width, STEP):
        for src in range(0, count, PIECE):
            inner = jnp.dot(
                source[src : src + PIECE, :AUG],
                target[:, first + col : first + col + STEP],
                preferred_element_type=f32,
            )
            if ready is not None:
                finish(*ready)
                ready = None
            if waiting is not None:
                ready = (waiting[0], waiting[1], gauss(waiting[2]))
            waiting = (col, src, inner)
    if ready is not None:
        finish(*ready)
    finish(waiting[0], waiting[1], gauss(waiting[2]))


def near_kernel(place, width, fresh, mask, block, *refs):
    if fresh:
        target, _, out, source = refs
    else:
        source, target, _, out = refs

    def tile():
        if fresh:
            source[...] = transposed(source_form(block[:DIM, :]))
        near_columns(source, block, target, out, width[0], width[1])

    if place is None:
        tile()
        return
    odd = lax.axis_index("leaf") % 2
    even_slot, odd_slot = SLOTS[place]
    wanted = jnp.where(odd == 1, mask[0, odd_slot], mask[0, even_slot]) > 0
    pl.when(wanted)(tile)

    @pl.when(jnp.logical_not(wanted))
    def _():
        out[...] = jnp.zeros_like(out)


def near(place, first, width, mask, block, source, target, token):
    fresh = source is None
    rows = block.shape[0] - DIM
    count = target.shape[1]
    arrays = (mask, block) + (() if fresh else (source,)) + (target, token)
    return pl.pallas_call(
        functools.partial(near_kernel, place, (first, width), fresh),
        out_shape=jax.ShapeDtypeStruct((rows, width), f32),
        in_specs=[SM] + [VM] * (len(arrays) - 2) + [ANY],
        out_specs=VM,
        scratch_shapes=[pltpu.VMEM((count, 128), bf16)] if fresh else [],
        compiler_params=params(),
        cost_estimate=pl.CostEstimate(flops=4 * 10**9 * width // count, bytes_accessed=10**6, transcendentals=0),
        name="near",
    )(*arrays)


def level_kernel(level, up, node, partner, token, half_t, parent):
    upper = (lax.axis_index("leaf") >> (level - 1)) & 1
    rank = node.shape[1]
    picks = up[level - 1]
    rows = lax.broadcasted_iota(jnp.int32, (rank, rank), 0)
    own_pick = jnp.where(rows + upper * rank == picks, 1.0, 0.0).astype(bf16)
    other_pick = jnp.where(rows + (1 - upper) * rank == picks, 1.0, 0.0).astype(bf16)
    own = node[:DIM, :]
    other = partner[:DIM, :]
    chosen = (
        jnp.dot(own, own_pick, preferred_element_type=f32)
        + jnp.dot(other, other_pick, preferred_element_type=f32)
    ).astype(bf16)
    chosen_tgt = target_form(chosen)
    own_half = interp_t(contract_rows(chosen_tgt, source_form(own)))
    other_half = interp_t(contract_rows(chosen_tgt, source_form(other)))
    half_t[...] = own_half
    charges = contract_cols(node[DIM:, :], own_half) + contract_cols(partner[DIM:, :], other_half)
    parent[:DIM, :] = chosen
    parent[DIM:, :] = charges.astype(bf16)


def climb(level, up, node, partner, token):
    rows, rank = node.shape
    return pl.pallas_call(
        functools.partial(level_kernel, level),
        out_shape=(
            jax.ShapeDtypeStruct((rank, rank), bf16),
            jax.ShapeDtypeStruct((rows, rank), bf16),
        ),
        in_specs=[VM, VM, VM, ANY],
        out_specs=(VM, VM),
        compiler_params=params(),
        name="climb",
    )(up, node, partner, token)


def couple_kernel(levels, *refs):
    for level in range(levels):
        node, partner, out = refs[level], refs[levels + level], refs[2 * levels + 1 + level]
        out[...] = coupling_of(node, partner)


def couple(nodes, partners, token):
    levels = len(nodes)
    rows, rank = nodes[0].shape
    return pl.pallas_call(
        functools.partial(couple_kernel, levels),
        out_shape=(jax.ShapeDtypeStruct((rows - DIM, rank), f32),) * levels,
        in_specs=[VM] * (2 * levels) + [ANY],
        out_specs=(VM,) * levels,
        compiler_params=params(),
        name="couple",
    )(*nodes, *partners, token)


def coupling_of(node, partner):
    kern = gauss(contract_rows(source_form(partner[:DIM, :]), target_form(node[:DIM, :])))
    return jnp.dot(partner[DIM:, :], kern, preferred_element_type=f32)


def top_kernel(levels, node, source, child, sibling, token, potential, coupling):
    place = lax.axis_index("leaf") & (2**levels - 1)
    potential[...] = jnp.where(place != 0, coupling_of(node, source), 0.0)
    coupling[...] = coupling_of(child, sibling)


def top(levels, node, source, child, sibling, token):
    rows, rank = node.shape
    return pl.pallas_call(
        functools.partial(top_kernel, levels),
        out_shape=(jax.ShapeDtypeStruct((rows - DIM, rank), f32),) * 2,
        in_specs=[VM, VM, VM, VM, ANY],
        out_specs=(VM, VM),
        compiler_params=params(),
        name="top",
    )(node, source, child, sibling, token)


def down_kernel(levels, starts, *refs):
    potential, last, weights_t = refs[:3]
    couplings = refs[3 : 3 + levels]
    halves = refs[3 + levels : 3 + 2 * levels]
    pieces = refs[3 + 2 * levels : -1]
    out = refs[-1]
    wave = potential[...] + last[...]
    for level in range(levels, 0, -1):
        wave = (
            jnp.dot(wave.astype(bf16), halves[level - 1][...], preferred_element_type=f32)
            + couplings[level - 1][...]
        )
    wave = wave.astype(bf16)
    for col in range(0, out.shape[1], STEP):
        total = None
        for start, piece in zip(starts, pieces):
            if start <= col < start + piece.shape[1]:
                part = piece[:, col - start : col - start + STEP]
                total = part if total is None else total + part
        far = jnp.dot(wave, weights_t[:, col : col + STEP], preferred_element_type=f32)
        out[:, col : col + STEP] = (total + far).astype(bf16)


def down(potential, last, weights_t, couplings, halves, pieces):
    levels = len(couplings)
    starts = [start for start, _ in pieces]
    arrays = (potential, last, weights_t, *couplings, *halves, *(p for _, p in pieces))
    return pl.pallas_call(
        functools.partial(down_kernel, levels, starts),
        out_shape=jax.ShapeDtypeStruct((potential.shape[0], weights_t.shape[1]), bf16),
        in_specs=[VM] * len(arrays),
        out_specs=VM,
        compiler_params=params(),
        name="down",
    )(*arrays)


def after(value, token):
    return lax.optimization_barrier((value, token))[0]


def top_target(i):
    core, low, high, x0 = (i >> bit & 1 for bit in range(4))
    return i ^ ((x0 | high << 1 | core << 2) << 5 | (low ^ high) << 4 or 16)


def body(points, charges, leaf_skel, up_skel, near_mask):
    levels = up_skel.shape[0]
    devices = lax.axis_size("leaf")
    pieces = []

    def send(value, target):
        pairs = [(i, target(i) % devices) for i in range(devices)]
        return lax.ppermute(value, "leaf", pairs)

    weights_t, node, block = leaf(points, charges, leaf_skel, first())
    nodes, partners, halves = [], [], []

    def exchange(mask):
        nodes.append(node)
        partners.append(send(node, lambda i: i ^ mask))

    def step(level, token):
        half_t, parent = climb(level, up_skel, nodes[-1], partners[-1], token)
        halves.append(half_t)
        return parent

    def piece(place, first_col, width, block, source, token):
        out = near(place, first_col, width, near_mask, block, source, target, token)
        pieces.append((first_col, out))
        return out

    exchange(1)
    mate = send(after(block, node), lambda i: i ^ 1)
    source, target = prep(block, node)
    node = step(1, target)
    exchange(2)
    across = send(after(block, node), lambda i: i + 1 if i % 2 else i - 1)
    token = piece(None, 0, 512, block, source, node)
    node = step(2, token)
    exchange(6)
    token = piece(None, 512, 1536, block, source, node)
    node = step(3, token)
    exchange(8)
    second = send(after(block, node), lambda i: i - 2 if i % 2 else i + 2)
    couplings = couple(nodes[:-1], partners[:-1], node)
    node = step(4, couplings[0])
    arrived = send(node, top_target)
    token = piece(0, 0, 2048, mate, None, node)
    passed = send(after(across, token), lambda i: i ^ 1)
    token = piece(1, 0, 768, across, None, token)
    wave, last_coupling = top(levels, node, arrived, nodes[-1], partners[-1], token)
    arrived = send(wave, lambda i: i ^ 1)
    wave = wave + arrived
    arrived = send(wave, lambda i: i ^ 2)
    token = piece(1, 768, 1280, across, None, wave)
    wave = wave + after(arrived, token)
    arrived = send(wave, lambda i: i ^ 6)
    token = piece(3, 0, 2048, passed, None, wave)
    wave = wave + after(arrived, token)
    arrived = send(wave, lambda i: i ^ 8)
    token = piece(2, 0, 2048, second, None, wave)
    return down(wave, arrived, weights_t, (*couplings, last_coupling), halves, pieces)


def solution(mesh):
    return jax.shard_map(
        body,
        mesh=mesh,
        in_specs=(
            P(None, "leaf"),
            P(None, "leaf"),
            P("leaf", None),
            P(None, "leaf", None),
            P("leaf", None),
        ),
        out_specs=P(None, "leaf"),
        check_vma=False,
    )
```

```python
import functools

import jax
import jax.numpy as jnp
from jax import lax
import jax.experimental.pallas as pl
import jax.experimental.pallas.tpu as pltpu
from jax.sharding import PartitionSpec as P

f32 = jnp.float32
bf16 = jnp.bfloat16
LOG2E = 1.4426950408889634
DIM = 64
STEP = 256
PIECE = 1024
AUG = 80


def params(mib=24):
    return pltpu.CompilerParams(vmem_limit_bytes=mib * 2**20)


VM = pl.BlockSpec(memory_space=pltpu.VMEM)
SM = pl.BlockSpec(memory_space=pltpu.SMEM)
ANY = pl.BlockSpec(memory_space=pl.ANY)

SLOTS = ((2, 1), (1, 2), (0, 3), (3, 0))


def norm_parts(pts):
    wide = pts.astype(f32)
    norm = jnp.sum(wide * wide, axis=0, keepdims=True)
    high = norm.astype(bf16).astype(f32)
    rest = norm - high
    mid = rest.astype(bf16).astype(f32)
    return high, mid, rest - mid


def extra_rows(first, second, count):
    row = lax.broadcasted_iota(jnp.int32, (16, count), 0)
    out = jnp.zeros((16, count), f32)
    for place, value in enumerate(tuple(first) + tuple(second)):
        out = jnp.where(row == place, value, out)
    return out.astype(bf16)


def source_form(pts):
    ones = (1.0, 1.0, 1.0)
    return jnp.concatenate([pts, extra_rows(norm_parts(pts), ones, pts.shape[1])], axis=0)


def target_form(pts):
    inv = 1.0 / DIM
    parts = norm_parts(pts)
    scaled = (pts.astype(f32) * (2.0 * inv)).astype(bf16)
    return jnp.concatenate(
        [scaled, extra_rows((-inv, -inv, -inv), [-inv * p for p in parts], pts.shape[1])], axis=0
    )


def contract_rows(left, right):
    return lax.dot_general(left, right, (((0,), (0,)), ((), ())), preferred_element_type=f32)


def contract_cols(left, right):
    return lax.dot_general(left, right, (((1,), (1,)), ((), ())), preferred_element_type=f32)


def gauss(neg_dist):
    return jnp.exp2(neg_dist * LOG2E).astype(bf16)


def interp_t(neg_dist):
    weight = 1.0 / (1.0 - neg_dist)
    total = jnp.sum(weight, axis=0, keepdims=True)
    return (weight * (1.0 / total)).astype(bf16)


def first_kernel(out):
    out[...] = jnp.zeros_like(out)


def first():
    return pl.pallas_call(
        first_kernel,
        out_shape=jax.ShapeDtypeStruct((8, 128), f32),
        out_specs=VM,
        compiler_params=params(),
        cost_estimate=pl.CostEstimate(flops=4 * 10**9, bytes_accessed=10**6, transcendentals=0),
        name="first",
    )()


def leaf_kernel(points, charges, skel, token, weights_t, node, block):
    pts = points[...]
    block[:DIM, :] = pts
    block[DIM:, :] = charges[...]
    rank = skel.shape[1]
    spots = lax.broadcasted_iota(jnp.int32, (pts.shape[1], rank), 0)
    pick = jnp.where(spots == skel[...], 1.0, 0.0).astype(bf16)
    chosen = jnp.dot(pts, pick, preferred_element_type=f32).astype(bf16)
    weights = interp_t(contract_rows(target_form(chosen), source_form(pts)))
    weights_t[...] = weights
    node[:DIM, :] = chosen
    node[DIM:, :] = contract_cols(charges[...], weights).astype(bf16)


def leaf(points, charges, skel, token):
    rank = skel.shape[1]
    count = points.shape[1]
    rows = DIM + charges.shape[0]
    return pl.pallas_call(
        leaf_kernel,
        out_shape=(
            jax.ShapeDtypeStruct((rank, count), bf16),
            jax.ShapeDtypeStruct((rows, rank), bf16),
            jax.ShapeDtypeStruct((rows, count), bf16),
        ),
        in_specs=[VM, VM, VM, ANY],
        out_specs=(VM, VM, VM),
        compiler_params=params(),
        name="leaf",
    )(points, charges, skel, token)


def transposed(form):
    count = form.shape[1]
    pad = jnp.zeros((128 - AUG, count), f32)
    return jnp.concatenate([form.astype(f32), pad], axis=0).T.astype(bf16)


def prep_kernel(block, token, source, target):
    pts = block[:DIM, :]
    source[...] = transposed(source_form(pts))
    target[...] = target_form(pts)


def prep(block, token):
    count = block.shape[1]
    return pl.pallas_call(
        prep_kernel,
        out_shape=(
            jax.ShapeDtypeStruct((count, 128), bf16),
            jax.ShapeDtypeStruct((AUG, count), bf16),
        ),
        in_specs=[VM, ANY],
        out_specs=(VM, VM),
        compiler_params=params(),
        name="prep",
    )(block, token)


def near_columns(source, charges, target, out, first, width):
    count = source.shape[0]
    waiting = ready = None
    sums = {}

    def finish(col, src, kern):
        part = jnp.dot(charges[DIM:, src : src + PIECE], kern, preferred_element_type=f32)
        sums[col] = part if src == 0 else sums[col] + part
        if src + PIECE == count:
            out[:, col : col + STEP] = sums.pop(col)

    for col in range(0, width, STEP):
        for src in range(0, count, PIECE):
            inner = jnp.dot(
                source[src : src + PIECE, :AUG],
                target[:, first + col : first + col + STEP],
                preferred_element_type=f32,
            )
            if ready is not None:
                finish(*ready)
                ready = None
            if waiting is not None:
                ready = (waiting[0], waiting[1], gauss(waiting[2]))
            waiting = (col, src, inner)
    if ready is not None:
        finish(*ready)
    finish(waiting[0], waiting[1], gauss(waiting[2]))


def near_kernel(place, width, fresh, mask, block, *refs):
    if fresh:
        target, _, out, source = refs
    else:
        source, target, _, out = refs

    def tile():
        if fresh:
            source[...] = transposed(source_form(block[:DIM, :]))
        near_columns(source, block, target, out, width[0], width[1])

    if place is None:
        tile()
        return
    odd = lax.axis_index("leaf") % 2
    even_slot, odd_slot = SLOTS[place]
    wanted = jnp.where(odd == 1, mask[0, odd_slot], mask[0, even_slot]) > 0
    pl.when(wanted)(tile)

    @pl.when(jnp.logical_not(wanted))
    def _():
        out[...] = jnp.zeros_like(out)


def near(place, first, width, mask, block, source, target, token):
    fresh = source is None
    rows = block.shape[0] - DIM
    count = target.shape[1]
    arrays = (mask, block) + (() if fresh else (source,)) + (target, token)
    return pl.pallas_call(
        functools.partial(near_kernel, place, (first, width), fresh),
        out_shape=jax.ShapeDtypeStruct((rows, width), f32),
        in_specs=[SM] + [VM] * (len(arrays) - 2) + [ANY],
        out_specs=VM,
        scratch_shapes=[pltpu.VMEM((count, 128), bf16)] if fresh else [],
        compiler_params=params(),
        cost_estimate=pl.CostEstimate(flops=4 * 10**9 * width // count, bytes_accessed=10**6, transcendentals=0),
        name="near",
    )(*arrays)


def self_kernel(block, source, target, token, out):
    count = source.shape[0]
    waiting = ready = None

    def finish(start, kern):
        part = jnp.dot(block[DIM:, start : start + STEP], kern, preferred_element_type=f32)
        out[:, start:] = part if start == 0 else out[:, start:] + part
        if start + STEP < count:
            out[:, start : start + STEP] += contract_cols(block[DIM:, start + STEP :], kern[:, STEP:])

    for start in range(0, count, STEP):
        inner = jnp.dot(
            source[start : start + STEP, :AUG], target[:, start:], preferred_element_type=f32
        )
        if ready is not None:
            finish(*ready)
            ready = None
        if waiting is not None:
            ready = (waiting[0], gauss(waiting[1]))
        waiting = (start, inner)
    if ready is not None:
        finish(*ready)
    finish(waiting[0], gauss(waiting[1]))


def near_self(block, source, target, token):
    count = source.shape[0]
    return pl.pallas_call(
        self_kernel,
        out_shape=jax.ShapeDtypeStruct((block.shape[0] - DIM, count), f32),
        in_specs=[VM, VM, VM, ANY],
        out_specs=VM,
        compiler_params=params(),
        cost_estimate=pl.CostEstimate(flops=4 * 10**9, bytes_accessed=10**6, transcendentals=0),
        name="near_self",
    )(block, source, target, token)


def level_kernel(level, up, node, partner, token, half_t, parent):
    upper = (lax.axis_index("leaf") >> (level - 1)) & 1
    rank = node.shape[1]
    picks = up[level - 1]
    rows = lax.broadcasted_iota(jnp.int32, (rank, rank), 0)
    own_pick = jnp.where(rows + upper * rank == picks, 1.0, 0.0).astype(bf16)
    other_pick = jnp.where(rows + (1 - upper) * rank == picks, 1.0, 0.0).astype(bf16)
    own = node[:DIM, :]
    other = partner[:DIM, :]
    chosen = (
        jnp.dot(own, own_pick, preferred_element_type=f32)
        + jnp.dot(other, other_pick, preferred_element_type=f32)
    ).astype(bf16)
    chosen_tgt = target_form(chosen)
    own_half = interp_t(contract_rows(chosen_tgt, source_form(own)))
    other_half = interp_t(contract_rows(chosen_tgt, source_form(other)))
    half_t[...] = own_half
    charges = contract_cols(node[DIM:, :], own_half) + contract_cols(partner[DIM:, :], other_half)
    parent[:DIM, :] = chosen
    parent[DIM:, :] = charges.astype(bf16)


def climb(level, up, node, partner, token):
    rows, rank = node.shape
    return pl.pallas_call(
        functools.partial(level_kernel, level),
        out_shape=(
            jax.ShapeDtypeStruct((rank, rank), bf16),
            jax.ShapeDtypeStruct((rows, rank), bf16),
        ),
        in_specs=[VM, VM, VM, ANY],
        out_specs=(VM, VM),
        compiler_params=params(),
        name="climb",
    )(up, node, partner, token)


def couple_kernel(levels, *refs):
    halves, weights_t = refs[2 * levels : 3 * levels], refs[3 * levels]
    constant, whole = refs[-2:]
    wave = path = None
    for level in range(levels - 1, -1, -1):
        node, partner, half = refs[level], refs[levels + level], halves[level][...]
        kern = gauss(contract_rows(source_form(partner[:DIM, :]), target_form(node[:DIM, :])))
        coupling = jnp.dot(partner[DIM:, :], kern, preferred_element_type=f32)
        if wave is None:
            wave, path = coupling, half
        else:
            wave = jnp.dot(wave.astype(bf16), half, preferred_element_type=f32) + coupling
            path = jnp.dot(path, half, preferred_element_type=f32).astype(bf16)
    constant[...] = jnp.dot(wave.astype(bf16), weights_t[...], preferred_element_type=f32)
    whole[...] = jnp.dot(path, weights_t[...], preferred_element_type=f32).astype(bf16)


def couple(nodes, partners, halves, weights_t, token):
    levels = len(nodes)
    rows, rank = nodes[0].shape
    count = weights_t.shape[1]
    return pl.pallas_call(
        functools.partial(couple_kernel, levels),
        out_shape=(
            jax.ShapeDtypeStruct((rows - DIM, count), f32),
            jax.ShapeDtypeStruct((rank, count), bf16),
        ),
        in_specs=[VM] * (3 * levels + 1) + [ANY],
        out_specs=(VM, VM),
        compiler_params=params(),
        cost_estimate=pl.CostEstimate(flops=4 * 10**9, bytes_accessed=10**6, transcendentals=0),
        name="couple",
    )(*nodes, *partners, *halves, weights_t, token)


def top_kernel(levels, node, source, token, potential):
    place = lax.axis_index("leaf") & (2**levels - 1)
    kern = gauss(contract_rows(source_form(source[:DIM, :]), target_form(node[:DIM, :])))
    part = jnp.dot(source[DIM:, :], kern, preferred_element_type=f32)
    potential[...] = jnp.where(place != 0, part, 0.0)


def top(levels, node, source, token):
    rows, rank = node.shape
    return pl.pallas_call(
        functools.partial(top_kernel, levels),
        out_shape=jax.ShapeDtypeStruct((rows - DIM, rank), f32),
        in_specs=[VM, VM, ANY],
        out_specs=VM,
        compiler_params=params(),
        name="top",
    )(node, source, token)


def down_kernel(starts, *refs):
    potential, last, constant, whole = refs[:4]
    pieces = refs[4:-1]
    out = refs[-1]
    wave = (potential[...] + last[...]).astype(bf16)
    for col in range(0, out.shape[1], STEP):
        total = constant[:, col : col + STEP]
        for start, piece in zip(starts, pieces):
            if start <= col < start + piece.shape[1]:
                total = total + piece[:, col - start : col - start + STEP]
        far = jnp.dot(wave, whole[:, col : col + STEP], preferred_element_type=f32)
        out[:, col : col + STEP] = (total + far).astype(bf16)


def down(potential, last, constant, whole, pieces):
    starts = [start for start, _ in pieces]
    arrays = (potential, last, constant, whole, *(p for _, p in pieces))
    return pl.pallas_call(
        functools.partial(down_kernel, starts),
        out_shape=jax.ShapeDtypeStruct(constant.shape, bf16),
        in_specs=[VM] * len(arrays),
        out_specs=VM,
        compiler_params=params(),
        name="down",
    )(*arrays)


def after(value, token):
    return lax.optimization_barrier((value, token))[0]


def top_target(i):
    core, low, high, x0 = (i >> bit & 1 for bit in range(4))
    return i ^ ((x0 | high << 1 | core << 2) << 5 | (low ^ high) << 4 or 16)


def body(points, charges, leaf_skel, up_skel, near_mask):
    levels = up_skel.shape[0]
    devices = lax.axis_size("leaf")
    pieces = []

    def send(value, target):
        pairs = [(i, target(i) % devices) for i in range(devices)]
        return lax.ppermute(value, "leaf", pairs)

    weights_t, node, block = leaf(points, charges, leaf_skel, first())
    nodes, partners, halves = [], [], []

    def exchange(mask):
        nodes.append(node)
        partners.append(send(node, lambda i: i ^ mask))

    def step(level, token):
        half_t, parent = climb(level, up_skel, nodes[-1], partners[-1], token)
        halves.append(half_t)
        return parent

    def piece(place, first_col, width, block, source, token):
        out = near(place, first_col, width, near_mask, block, source, target, token)
        pieces.append((first_col, out))
        return out

    exchange(1)
    mate = send(after(block, node), lambda i: i ^ 1)
    source, target = prep(block, node)
    node = step(1, target)
    exchange(2)
    token = near_self(block, source, target, node)
    pieces.append((0, token))
    node = step(2, token)
    exchange(6)
    token = piece(0, 0, 2048, mate, None, node)
    node = step(3, token)
    exchange(8)
    sent = after(block, node)
    across = send(sent, lambda i: i + 1 if i % 2 else i - 1)
    second = send(sent, lambda i: i - 2 if i % 2 else i + 2)
    node = step(4, node)
    constant, whole = couple(nodes, partners, halves, weights_t, node)
    arrived = send(node, top_target)
    passed = send(after(across, node), lambda i: i ^ 1)
    wave = top(levels, node, arrived, constant)
    arrived = send(wave, lambda i: i ^ 1)
    wave = wave + arrived
    arrived = send(wave, lambda i: i ^ 2)
    token = piece(1, 0, 2048, across, None, wave)
    wave = wave + after(arrived, token)
    arrived = send(wave, lambda i: i ^ 6)
    token = piece(2, 0, 2048, second, None, wave)
    wave = wave + after(arrived, token)
    arrived = send(wave, lambda i: i ^ 8)
    token = piece(3, 0, 2048, passed, None, wave)
    return down(wave, arrived, constant, whole, pieces)


def solution(mesh):
    return jax.shard_map(
        body,
        mesh=mesh,
        in_specs=(
            P(None, "leaf"),
            P(None, "leaf"),
            P("leaf", None),
            P(None, "leaf", None),
            P("leaf", None),
        ),
        out_specs=P(None, "leaf"),
        check_vma=False,
    )
```

```python
import functools

import jax
import jax.numpy as jnp
from jax import lax
import jax.experimental.pallas as pl
import jax.experimental.pallas.tpu as pltpu
from jax.sharding import PartitionSpec as P

f32 = jnp.float32
bf16 = jnp.bfloat16
LOG2E = 1.4426950408889634
DIM = 64
STEP = 256
PIECE = 1024
AUG = 80


def params(mib=24):
    return pltpu.CompilerParams(vmem_limit_bytes=mib * 2**20)


VM = pl.BlockSpec(memory_space=pltpu.VMEM)
SM = pl.BlockSpec(memory_space=pltpu.SMEM)
ANY = pl.BlockSpec(memory_space=pl.ANY)

SLOTS = ((2, 1), (1, 2), (0, 3), (3, 0))


def norm_parts(pts):
    wide = pts.astype(f32)
    norm = jnp.sum(wide * wide, axis=0, keepdims=True)
    high = norm.astype(bf16).astype(f32)
    rest = norm - high
    mid = rest.astype(bf16).astype(f32)
    return high, mid, rest - mid


def extra_rows(first, second, count):
    row = lax.broadcasted_iota(jnp.int32, (16, count), 0)
    out = jnp.zeros((16, count), f32)
    for place, value in enumerate(tuple(first) + tuple(second)):
        out = jnp.where(row == place, value, out)
    return out.astype(bf16)


def source_form(pts):
    ones = (1.0, 1.0, 1.0)
    return jnp.concatenate([pts, extra_rows(norm_parts(pts), ones, pts.shape[1])], axis=0)


def target_form(pts):
    inv = 1.0 / DIM
    parts = norm_parts(pts)
    scaled = (pts.astype(f32) * (2.0 * inv)).astype(bf16)
    return jnp.concatenate(
        [scaled, extra_rows((-inv, -inv, -inv), [-inv * p for p in parts], pts.shape[1])], axis=0
    )


def contract_rows(left, right):
    return lax.dot_general(left, right, (((0,), (0,)), ((), ())), preferred_element_type=f32)


def contract_cols(left, right):
    return lax.dot_general(left, right, (((1,), (1,)), ((), ())), preferred_element_type=f32)


def gauss(neg_dist):
    return jnp.exp2(neg_dist * LOG2E).astype(bf16)


def interp_t(neg_dist):
    weight = 1.0 / (1.0 - neg_dist)
    total = jnp.sum(weight, axis=0, keepdims=True)
    return (weight * (1.0 / total)).astype(bf16)


def first_kernel(out):
    out[...] = jnp.zeros_like(out)


def first():
    return pl.pallas_call(
        first_kernel,
        out_shape=jax.ShapeDtypeStruct((8, 128), f32),
        out_specs=VM,
        compiler_params=params(),
        cost_estimate=pl.CostEstimate(flops=4 * 10**9, bytes_accessed=10**6, transcendentals=0),
        name="first",
    )()


def leaf_kernel(points, charges, skel, token, weights_t, node, block):
    pts = points[...]
    block[:DIM, :] = pts
    block[DIM:, :] = charges[...]
    rank = skel.shape[1]
    spots = lax.broadcasted_iota(jnp.int32, (pts.shape[1], rank), 0)
    pick = jnp.where(spots == skel[...], 1.0, 0.0).astype(bf16)
    chosen = jnp.dot(pts, pick, preferred_element_type=f32).astype(bf16)
    weights = interp_t(contract_rows(target_form(chosen), source_form(pts)))
    weights_t[...] = weights
    node[:DIM, :] = chosen
    node[DIM:, :] = contract_cols(charges[...], weights).astype(bf16)


def leaf(points, charges, skel, token):
    rank = skel.shape[1]
    count = points.shape[1]
    rows = DIM + charges.shape[0]
    return pl.pallas_call(
        leaf_kernel,
        out_shape=(
            jax.ShapeDtypeStruct((rank, count), bf16),
            jax.ShapeDtypeStruct((rows, rank), bf16),
            jax.ShapeDtypeStruct((rows, count), bf16),
        ),
        in_specs=[VM, VM, VM, ANY],
        out_specs=(VM, VM, VM),
        compiler_params=params(),
        name="leaf",
    )(points, charges, skel, token)


def transposed(form):
    count = form.shape[1]
    pad = jnp.zeros((128 - AUG, count), f32)
    return jnp.concatenate([form.astype(f32), pad], axis=0).T.astype(bf16)


def prep_kernel(block, token, source, target):
    pts = block[:DIM, :]
    source[...] = transposed(source_form(pts))
    target[...] = target_form(pts)


def prep(block, token):
    count = block.shape[1]
    return pl.pallas_call(
        prep_kernel,
        out_shape=(
            jax.ShapeDtypeStruct((count, 128), bf16),
            jax.ShapeDtypeStruct((AUG, count), bf16),
        ),
        in_specs=[VM, ANY],
        out_specs=(VM, VM),
        compiler_params=params(),
        name="prep",
    )(block, token)


def near_columns(source, charges, target, out, first, width):
    count = source.shape[0]
    waiting = ready = None
    sums = {}

    def finish(col, src, kern):
        part = jnp.dot(charges[DIM:, src : src + PIECE], kern, preferred_element_type=f32)
        sums[col] = part if src == 0 else sums[col] + part
        if src + PIECE == count:
            out[:, col : col + STEP] = sums.pop(col)

    for col in range(0, width, STEP):
        for src in range(0, count, PIECE):
            inner = jnp.dot(
                source[src : src + PIECE, :AUG],
                target[:, first + col : first + col + STEP],
                preferred_element_type=f32,
            )
            if ready is not None:
                finish(*ready)
                ready = None
            if waiting is not None:
                ready = (waiting[0], waiting[1], gauss(waiting[2]))
            waiting = (col, src, inner)
    if ready is not None:
        finish(*ready)
    finish(waiting[0], waiting[1], gauss(waiting[2]))


def near_kernel(place, width, fresh, mask, block, *refs):
    if fresh:
        target, _, out, source = refs
    else:
        source, target, _, out = refs

    def tile():
        if fresh:
            source[...] = transposed(source_form(block[:DIM, :]))
        near_columns(source, block, target, out, width[0], width[1])

    if place is None:
        tile()
        return
    odd = lax.axis_index("leaf") % 2
    even_slot, odd_slot = SLOTS[place]
    wanted = jnp.where(odd == 1, mask[0, odd_slot], mask[0, even_slot]) > 0
    pl.when(wanted)(tile)

    @pl.when(jnp.logical_not(wanted))
    def _():
        out[...] = jnp.zeros_like(out)


def near(place, first, width, mask, block, source, target, token):
    fresh = source is None
    rows = block.shape[0] - DIM
    count = target.shape[1]
    arrays = (mask, block) + (() if fresh else (source,)) + (target, token)
    return pl.pallas_call(
        functools.partial(near_kernel, place, (first, width), fresh),
        out_shape=jax.ShapeDtypeStruct((rows, width), f32),
        in_specs=[SM] + [VM] * (len(arrays) - 2) + [ANY],
        out_specs=VM,
        scratch_shapes=[pltpu.VMEM((count, 128), bf16)] if fresh else [],
        compiler_params=params(),
        cost_estimate=pl.CostEstimate(flops=(5 if place == 3 else 40) * 10**8 * width // count, bytes_accessed=10**6, transcendentals=0),
        name="near",
    )(*arrays)


def self_kernel(block, source, target, token, out):
    count = source.shape[0]
    waiting = ready = None

    def finish(start, kern):
        part = jnp.dot(block[DIM:, start : start + STEP], kern, preferred_element_type=f32)
        out[:, start:] = part if start == 0 else out[:, start:] + part
        if start + STEP < count:
            out[:, start : start + STEP] += contract_cols(block[DIM:, start + STEP :], kern[:, STEP:])

    for start in range(0, count, STEP):
        inner = jnp.dot(
            source[start : start + STEP, :AUG], target[:, start:], preferred_element_type=f32
        )
        if ready is not None:
            finish(*ready)
            ready = None
        if waiting is not None:
            ready = (waiting[0], gauss(waiting[1]))
        waiting = (start, inner)
    if ready is not None:
        finish(*ready)
    finish(waiting[0], gauss(waiting[1]))


def near_self(block, source, target, token):
    count = source.shape[0]
    return pl.pallas_call(
        self_kernel,
        out_shape=jax.ShapeDtypeStruct((block.shape[0] - DIM, count), f32),
        in_specs=[VM, VM, VM, ANY],
        out_specs=VM,
        compiler_params=params(),
        cost_estimate=pl.CostEstimate(flops=4 * 10**9, bytes_accessed=10**6, transcendentals=0),
        name="near_self",
    )(block, source, target, token)


def level_kernel(level, up, node, partner, token, half_t, parent):
    upper = (lax.axis_index("leaf") >> (level - 1)) & 1
    rank = node.shape[1]
    picks = up[level - 1]
    rows = lax.broadcasted_iota(jnp.int32, (rank, rank), 0)
    own_pick = jnp.where(rows + upper * rank == picks, 1.0, 0.0).astype(bf16)
    other_pick = jnp.where(rows + (1 - upper) * rank == picks, 1.0, 0.0).astype(bf16)
    own = node[:DIM, :]
    other = partner[:DIM, :]
    chosen = (
        jnp.dot(own, own_pick, preferred_element_type=f32)
        + jnp.dot(other, other_pick, preferred_element_type=f32)
    ).astype(bf16)
    chosen_tgt = target_form(chosen)
    own_half = interp_t(contract_rows(chosen_tgt, source_form(own)))
    other_half = interp_t(contract_rows(chosen_tgt, source_form(other)))
    half_t[...] = own_half
    charges = contract_cols(node[DIM:, :], own_half) + contract_cols(partner[DIM:, :], other_half)
    parent[:DIM, :] = chosen
    parent[DIM:, :] = charges.astype(bf16)


def climb(level, up, node, partner, token):
    rows, rank = node.shape
    return pl.pallas_call(
        functools.partial(level_kernel, level),
        out_shape=(
            jax.ShapeDtypeStruct((rank, rank), bf16),
            jax.ShapeDtypeStruct((rows, rank), bf16),
        ),
        in_specs=[VM, VM, VM, ANY],
        out_specs=(VM, VM),
        compiler_params=params(),
        name="climb",
    )(up, node, partner, token)


def couple_kernel(levels, *refs):
    halves, weights_t = refs[2 * levels : 3 * levels], refs[3 * levels]
    constant, whole = refs[-2:]
    wave = path = None
    for level in range(levels - 1, -1, -1):
        node, partner, half = refs[level], refs[levels + level], halves[level][...]
        kern = gauss(contract_rows(source_form(partner[:DIM, :]), target_form(node[:DIM, :])))
        coupling = jnp.dot(partner[DIM:, :], kern, preferred_element_type=f32)
        if wave is None:
            wave, path = coupling, half
        else:
            wave = jnp.dot(wave.astype(bf16), half, preferred_element_type=f32) + coupling
            path = jnp.dot(path, half, preferred_element_type=f32).astype(bf16)
    constant[...] = jnp.dot(wave.astype(bf16), weights_t[...], preferred_element_type=f32)
    whole[...] = jnp.dot(path, weights_t[...], preferred_element_type=f32).astype(bf16)


def couple(nodes, partners, halves, weights_t, token):
    levels = len(nodes)
    rows, rank = nodes[0].shape
    count = weights_t.shape[1]
    return pl.pallas_call(
        functools.partial(couple_kernel, levels),
        out_shape=(
            jax.ShapeDtypeStruct((rows - DIM, count), f32),
            jax.ShapeDtypeStruct((rank, count), bf16),
        ),
        in_specs=[VM] * (3 * levels + 1) + [ANY],
        out_specs=(VM, VM),
        compiler_params=params(),
        cost_estimate=pl.CostEstimate(flops=4 * 10**9, bytes_accessed=10**6, transcendentals=0),
        name="couple",
    )(*nodes, *partners, *halves, weights_t, token)


def top_kernel(levels, node, source, token, potential):
    place = lax.axis_index("leaf") & (2**levels - 1)
    kern = gauss(contract_rows(source_form(source[:DIM, :]), target_form(node[:DIM, :])))
    part = jnp.dot(source[DIM:, :], kern, preferred_element_type=f32)
    potential[...] = jnp.where(place != 0, part, 0.0)


def top(levels, node, source, token):
    rows, rank = node.shape
    return pl.pallas_call(
        functools.partial(top_kernel, levels),
        out_shape=jax.ShapeDtypeStruct((rows - DIM, rank), f32),
        in_specs=[VM, VM, ANY],
        out_specs=VM,
        compiler_params=params(),
        name="top",
    )(node, source, token)


def down_kernel(starts, *refs):
    potential, last, constant, whole = refs[:4]
    pieces = refs[4:-1]
    out = refs[-1]
    wave = (potential[...] + last[...]).astype(bf16)
    for col in range(0, out.shape[1], STEP):
        total = constant[:, col : col + STEP]
        for start, piece in zip(starts, pieces):
            if start <= col < start + piece.shape[1]:
                total = total + piece[:, col - start : col - start + STEP]
        far = jnp.dot(wave, whole[:, col : col + STEP], preferred_element_type=f32)
        out[:, col : col + STEP] = (total + far).astype(bf16)


def down(potential, last, constant, whole, pieces):
    starts = [start for start, _ in pieces]
    arrays = (potential, last, constant, whole, *(p for _, p in pieces))
    return pl.pallas_call(
        functools.partial(down_kernel, starts),
        out_shape=jax.ShapeDtypeStruct(constant.shape, bf16),
        in_specs=[VM] * len(arrays),
        out_specs=VM,
        compiler_params=params(),
        name="down",
    )(*arrays)


def after(value, token):
    return lax.optimization_barrier((value, token))[0]


def top_target(i):
    core, low, high, x0 = (i >> bit & 1 for bit in range(4))
    return i ^ ((x0 | high << 1 | core << 2) << 5 | (low ^ high) << 4 or 16)


def body(points, charges, leaf_skel, up_skel, near_mask):
    levels = up_skel.shape[0]
    devices = lax.axis_size("leaf")
    pieces = []

    def two_on(i):
        to = i - 2 if i % 2 else i + 2
        return to if 0 <= to < devices else i ^ 1

    def send(value, target):
        pairs = [(i, target(i) % devices) for i in range(devices)]
        return lax.ppermute(value, "leaf", pairs)

    weights_t, node, block = leaf(points, charges, leaf_skel, first())
    nodes, partners, halves = [], [], []

    def exchange(mask):
        nodes.append(node)
        partners.append(send(node, lambda i: i ^ mask))

    def step(level, token):
        half_t, parent = climb(level, up_skel, nodes[-1], partners[-1], token)
        halves.append(half_t)
        return parent

    def piece(place, first_col, width, block, source, token):
        out = near(place, first_col, width, near_mask, block, source, target, token)
        pieces.append((first_col, out))
        return out

    exchange(1)
    mate = send(after(block, node), lambda i: i ^ 1)
    source, target = prep(block, node)
    node = step(1, target)
    exchange(2)
    token = near_self(block, source, target, node)
    pieces.append((0, token))
    node = step(2, token)
    exchange(6)
    token = piece(0, 0, 2048, mate, None, node)
    node = step(3, token)
    exchange(8)
    sent = after(block, node)
    across = send(sent, lambda i: i + 1 if i % 2 else i - 1)
    second = send(sent, two_on)
    node = step(4, node)
    constant, whole = couple(nodes, partners, halves, weights_t, node)
    arrived = send(node, top_target)
    passed = send(after(across, node), lambda i: i ^ 1)
    wave = top(levels, node, arrived, constant)
    arrived = send(wave, lambda i: i ^ 1)
    wave = wave + arrived
    arrived = send(wave, lambda i: i ^ 8)
    token = piece(1, 0, 2048, across, None, wave)
    wave = wave + after(arrived, token)
    arrived = send(wave, lambda i: i ^ 2)
    token = piece(3, 0, 2048, passed, None, wave)
    wave = wave + after(arrived, token)
    arrived = send(wave, lambda i: i ^ 6)
    token = piece(2, 0, 2048, second, None, wave)
    return down(wave, arrived, constant, whole, pieces)


def solution(mesh):
    return jax.shard_map(
        body,
        mesh=mesh,
        in_specs=(
            P(None, "leaf"),
            P(None, "leaf"),
            P("leaf", None),
            P(None, "leaf", None),
            P("leaf", None),
        ),
        out_specs=P(None, "leaf"),
        check_vma=False,
    )
```

```python
import functools

import jax
import jax.numpy as jnp
from jax import lax
import jax.experimental.pallas as pl
import jax.experimental.pallas.tpu as pltpu
from jax.sharding import PartitionSpec as P

f32 = jnp.float32
bf16 = jnp.bfloat16
LOG2E = 1.4426950408889634
DIM = 64
STEP = 256
PIECE = 1024
AUG = 80


def params(mib=24):
    return pltpu.CompilerParams(vmem_limit_bytes=mib * 2**20)


VM = pl.BlockSpec(memory_space=pltpu.VMEM)
SM = pl.BlockSpec(memory_space=pltpu.SMEM)
ANY = pl.BlockSpec(memory_space=pl.ANY)

SLOTS = ((2, 1), (1, 2), (0, 3), (3, 0))


def norm_parts(pts):
    wide = pts.astype(f32)
    norm = jnp.sum(wide * wide, axis=0, keepdims=True)
    high = norm.astype(bf16).astype(f32)
    rest = norm - high
    mid = rest.astype(bf16).astype(f32)
    return high, mid, rest - mid


def extra_rows(first, second, count):
    row = lax.broadcasted_iota(jnp.int32, (16, count), 0)
    out = jnp.zeros((16, count), f32)
    for place, value in enumerate(tuple(first) + tuple(second)):
        out = jnp.where(row == place, value, out)
    return out.astype(bf16)


def source_form(pts):
    ones = (1.0, 1.0, 1.0)
    return jnp.concatenate([pts, extra_rows(norm_parts(pts), ones, pts.shape[1])], axis=0)


def target_form(pts):
    inv = 1.0 / DIM
    parts = norm_parts(pts)
    scaled = (pts.astype(f32) * (2.0 * inv)).astype(bf16)
    return jnp.concatenate(
        [scaled, extra_rows((-inv, -inv, -inv), [-inv * p for p in parts], pts.shape[1])], axis=0
    )


def contract_rows(left, right):
    return lax.dot_general(left, right, (((0,), (0,)), ((), ())), preferred_element_type=f32)


def contract_cols(left, right):
    return lax.dot_general(left, right, (((1,), (1,)), ((), ())), preferred_element_type=f32)


def gauss(neg_dist):
    return jnp.exp2(neg_dist * LOG2E).astype(bf16)


def interp_t(neg_dist):
    weight = 1.0 / (1.0 - neg_dist)
    total = jnp.sum(weight, axis=0, keepdims=True)
    return (weight * (1.0 / total)).astype(bf16)


def first_kernel(out):
    out[...] = jnp.zeros_like(out)


def first():
    return pl.pallas_call(
        first_kernel,
        out_shape=jax.ShapeDtypeStruct((8, 128), f32),
        out_specs=VM,
        compiler_params=params(),
        cost_estimate=pl.CostEstimate(flops=4 * 10**9, bytes_accessed=10**6, transcendentals=0),
        name="first",
    )()


def leaf_kernel(points, charges, skel, token, weights_t, node, block):
    pts = points[...]
    block[:DIM, :] = pts
    block[DIM:, :] = charges[...]
    rank = skel.shape[1]
    spots = lax.broadcasted_iota(jnp.int32, (pts.shape[1], rank), 0)
    pick = jnp.where(spots == skel[...], 1.0, 0.0).astype(bf16)
    chosen = jnp.dot(pts, pick, preferred_element_type=f32).astype(bf16)
    weights = interp_t(contract_rows(target_form(chosen), source_form(pts)))
    weights_t[...] = weights
    node[:DIM, :] = chosen
    node[DIM:, :] = contract_cols(charges[...], weights).astype(bf16)


def leaf(points, charges, skel, token):
    rank = skel.shape[1]
    count = points.shape[1]
    rows = DIM + charges.shape[0]
    return pl.pallas_call(
        leaf_kernel,
        out_shape=(
            jax.ShapeDtypeStruct((rank, count), bf16),
            jax.ShapeDtypeStruct((rows, rank), bf16),
            jax.ShapeDtypeStruct((rows, count), bf16),
        ),
        in_specs=[VM, VM, VM, ANY],
        out_specs=(VM, VM, VM),
        compiler_params=params(),
        name="leaf",
    )(points, charges, skel, token)


def transposed(form):
    count = form.shape[1]
    pad = jnp.zeros((128 - AUG, count), f32)
    return jnp.concatenate([form.astype(f32), pad], axis=0).T.astype(bf16)


def prep_kernel(block, token, source, target):
    pts = block[:DIM, :]
    source[...] = transposed(source_form(pts))
    target[...] = target_form(pts)


def prep(block, token):
    count = block.shape[1]
    return pl.pallas_call(
        prep_kernel,
        out_shape=(
            jax.ShapeDtypeStruct((count, 128), bf16),
            jax.ShapeDtypeStruct((AUG, count), bf16),
        ),
        in_specs=[VM, ANY],
        out_specs=(VM, VM),
        compiler_params=params(),
        name="prep",
    )(block, token)


def near_columns(source, charges, target, out, first, width):
    count = source.shape[0]
    waiting = ready = None
    sums = {}

    def finish(col, src, kern):
        part = jnp.dot(charges[DIM:, src : src + PIECE], kern, preferred_element_type=f32)
        sums[col] = part if src == 0 else sums[col] + part
        if src + PIECE == count:
            out[:, col : col + STEP] = sums.pop(col)

    for col in range(0, width, STEP):
        for src in range(0, count, PIECE):
            inner = jnp.dot(
                source[src : src + PIECE, :AUG],
                target[:, first + col : first + col + STEP],
                preferred_element_type=f32,
            )
            if ready is not None:
                finish(*ready)
                ready = None
            if waiting is not None:
                ready = (waiting[0], waiting[1], gauss(waiting[2]))
            waiting = (col, src, inner)
    if ready is not None:
        finish(*ready)
    finish(waiting[0], waiting[1], gauss(waiting[2]))


def near_kernel(place, width, fresh, mask, block, *refs):
    if fresh:
        target, _, out, source = refs
    else:
        source, target, _, out = refs

    def tile():
        if fresh:
            source[...] = transposed(source_form(block[:DIM, :]))
        near_columns(source, block, target, out, width[0], width[1])

    if place is None:
        tile()
        return
    odd = lax.axis_index("leaf") % 2
    even_slot, odd_slot = SLOTS[place]
    wanted = jnp.where(odd == 1, mask[0, odd_slot], mask[0, even_slot]) > 0
    pl.when(wanted)(tile)

    @pl.when(jnp.logical_not(wanted))
    def _():
        out[...] = jnp.zeros_like(out)


def near(place, first, width, mask, block, source, target, token):
    fresh = source is None
    rows = block.shape[0] - DIM
    count = target.shape[1]
    arrays = (mask, block) + (() if fresh else (source,)) + (target, token)
    return pl.pallas_call(
        functools.partial(near_kernel, place, (first, width), fresh),
        out_shape=jax.ShapeDtypeStruct((rows, width), f32),
        in_specs=[SM] + [VM] * (len(arrays) - 2) + [ANY],
        out_specs=VM,
        scratch_shapes=[pltpu.VMEM((count, 128), bf16)] if fresh else [],
        compiler_params=params(),
        cost_estimate=pl.CostEstimate(flops=(5 if place == 3 else 40) * 10**8 * width // count, bytes_accessed=10**6, transcendentals=0),
        name="near",
    )(*arrays)


def self_kernel(block, source, target, token, out):
    count = source.shape[0]
    waiting = ready = None

    def finish(start, kern):
        part = jnp.dot(block[DIM:, start : start + STEP], kern, preferred_element_type=f32)
        out[:, start:] = part if start == 0 else out[:, start:] + part
        if start + STEP < count:
            out[:, start : start + STEP] += contract_cols(block[DIM:, start + STEP :], kern[:, STEP:])

    for start in range(0, count, STEP):
        inner = jnp.dot(
            source[start : start + STEP, :AUG], target[:, start:], preferred_element_type=f32
        )
        if ready is not None:
            finish(*ready)
            ready = None
        if waiting is not None:
            ready = (waiting[0], gauss(waiting[1]))
        waiting = (start, inner)
    if ready is not None:
        finish(*ready)
    finish(waiting[0], gauss(waiting[1]))


def near_self(block, source, target, token):
    count = source.shape[0]
    return pl.pallas_call(
        self_kernel,
        out_shape=jax.ShapeDtypeStruct((block.shape[0] - DIM, count), f32),
        in_specs=[VM, VM, VM, ANY],
        out_specs=VM,
        compiler_params=params(),
        cost_estimate=pl.CostEstimate(flops=4 * 10**9, bytes_accessed=10**6, transcendentals=0),
        name="near_self",
    )(block, source, target, token)


def level_kernel(level, up, node, partner, token, half_t, parent):
    upper = (lax.axis_index("leaf") >> (level - 1)) & 1
    rank = node.shape[1]
    picks = up[level - 1]
    rows = lax.broadcasted_iota(jnp.int32, (rank, rank), 0)
    own_pick = jnp.where(rows + upper * rank == picks, 1.0, 0.0).astype(bf16)
    other_pick = jnp.where(rows + (1 - upper) * rank == picks, 1.0, 0.0).astype(bf16)
    own = node[:DIM, :]
    other = partner[:DIM, :]
    chosen = (
        jnp.dot(own, own_pick, preferred_element_type=f32)
        + jnp.dot(other, other_pick, preferred_element_type=f32)
    ).astype(bf16)
    chosen_tgt = target_form(chosen)
    own_half = interp_t(contract_rows(chosen_tgt, source_form(own)))
    other_half = interp_t(contract_rows(chosen_tgt, source_form(other)))
    half_t[...] = own_half
    charges = contract_cols(node[DIM:, :], own_half) + contract_cols(partner[DIM:, :], other_half)
    parent[:DIM, :] = chosen
    parent[DIM:, :] = charges.astype(bf16)


def climb(level, up, node, partner, token):
    rows, rank = node.shape
    return pl.pallas_call(
        functools.partial(level_kernel, level),
        out_shape=(
            jax.ShapeDtypeStruct((rank, rank), bf16),
            jax.ShapeDtypeStruct((rows, rank), bf16),
        ),
        in_specs=[VM, VM, VM, ANY],
        out_specs=(VM, VM),
        compiler_params=params(),
        name="climb",
    )(up, node, partner, token)


def couple_kernel(levels, *refs):
    halves, weights_t = refs[2 * levels : 3 * levels], refs[3 * levels]
    constant, whole = refs[-2:]
    wave = path = None
    for level in range(levels - 1, -1, -1):
        node, partner, half = refs[level], refs[levels + level], halves[level][...]
        kern = gauss(contract_rows(source_form(partner[:DIM, :]), target_form(node[:DIM, :])))
        coupling = jnp.dot(partner[DIM:, :], kern, preferred_element_type=f32)
        if wave is None:
            wave, path = coupling, half
        else:
            wave = jnp.dot(wave.astype(bf16), half, preferred_element_type=f32) + coupling
            path = jnp.dot(path, half, preferred_element_type=f32).astype(bf16)
    constant[...] = jnp.dot(wave.astype(bf16), weights_t[...], preferred_element_type=f32)
    whole[...] = jnp.dot(path, weights_t[...], preferred_element_type=f32).astype(bf16)


def couple(nodes, partners, halves, weights_t, token):
    levels = len(nodes)
    rows, rank = nodes[0].shape
    count = weights_t.shape[1]
    return pl.pallas_call(
        functools.partial(couple_kernel, levels),
        out_shape=(
            jax.ShapeDtypeStruct((rows - DIM, count), f32),
            jax.ShapeDtypeStruct((rank, count), bf16),
        ),
        in_specs=[VM] * (3 * levels + 1) + [ANY],
        out_specs=(VM, VM),
        compiler_params=params(),
        cost_estimate=pl.CostEstimate(flops=4 * 10**9, bytes_accessed=10**6, transcendentals=0),
        name="couple",
    )(*nodes, *partners, *halves, weights_t, token)


def top_kernel(levels, node, source, token, potential):
    place = lax.axis_index("leaf") & (2**levels - 1)
    kern = gauss(contract_rows(source_form(source[:DIM, :]), target_form(node[:DIM, :])))
    part = jnp.dot(source[DIM:, :], kern, preferred_element_type=f32)
    potential[...] = jnp.where(place != 0, part, 0.0)


def top(levels, node, source, token):
    rows, rank = node.shape
    return pl.pallas_call(
        functools.partial(top_kernel, levels),
        out_shape=jax.ShapeDtypeStruct((rows - DIM, rank), f32),
        in_specs=[VM, VM, ANY],
        out_specs=VM,
        compiler_params=params(),
        name="top",
    )(node, source, token)


def down_kernel(starts, *refs):
    potential, last, constant, whole = refs[:4]
    pieces = refs[4:-1]
    out = refs[-1]
    wave = (potential[...] + last[...]).astype(bf16)
    for col in range(0, out.shape[1], STEP):
        total = constant[:, col : col + STEP]
        for start, piece in zip(starts, pieces):
            if start <= col < start + piece.shape[1]:
                total = total + piece[:, col - start : col - start + STEP]
        far = jnp.dot(wave, whole[:, col : col + STEP], preferred_element_type=f32)
        out[:, col : col + STEP] = (total + far).astype(bf16)


def down(potential, last, constant, whole, pieces):
    starts = [start for start, _ in pieces]
    arrays = (potential, last, constant, whole, *(p for _, p in pieces))
    return pl.pallas_call(
        functools.partial(down_kernel, starts),
        out_shape=jax.ShapeDtypeStruct(constant.shape, bf16),
        in_specs=[VM] * len(arrays),
        out_specs=VM,
        compiler_params=params(),
        name="down",
    )(*arrays)


def after(value, token):
    return lax.optimization_barrier((value, token))[0]


def top_target(i):
    core, low, high, x0 = (i >> bit & 1 for bit in range(4))
    return i ^ ((x0 | high << 1 | core << 2) << 5 | (low ^ high) << 4 or 16)


def body(points, charges, leaf_skel, up_skel, near_mask):
    levels = up_skel.shape[0]
    devices = lax.axis_size("leaf")
    pieces = []

    def two_on(i):
        to = i - 2 if i % 2 else i + 2
        return to if 0 <= to < devices else i ^ 1

    def send(value, target):
        pairs = [(i, target(i) % devices) for i in range(devices)]
        return lax.ppermute(value, "leaf", pairs)

    weights_t, node, block = leaf(points, charges, leaf_skel, first())
    nodes, partners, halves = [], [], []

    def exchange(mask):
        nodes.append(node)
        partners.append(send(node, lambda i: i ^ mask))

    def step(level, token):
        half_t, parent = climb(level, up_skel, nodes[-1], partners[-1], token)
        halves.append(half_t)
        return parent

    def piece(place, first_col, width, block, source, token):
        out = near(place, first_col, width, near_mask, block, source, target, token)
        pieces.append((first_col, out))
        return out

    exchange(1)
    mate = send(after(block, node), lambda i: i ^ 1)
    source, target = prep(block, node)
    node = step(1, target)
    exchange(2)
    token = near_self(block, source, target, node)
    pieces.append((0, token))
    node = step(2, token)
    exchange(6)
    token = piece(0, 0, 1280, mate, None, node)
    node = step(3, token)
    exchange(8)
    sent = after(block, node)
    across = send(sent, lambda i: i + 1 if i % 2 else i - 1)
    second = send(sent, two_on)
    node = step(4, node)
    constant, whole = couple(nodes, partners, halves, weights_t, node)
    arrived = send(node, top_target)
    passed = send(after(across, node), lambda i: i ^ 1)
    token = piece(0, 1280, 768, mate, None, constant)
    wave = top(levels, node, arrived, token)
    arrived = send(wave, lambda i: i ^ 1)
    wave = wave + arrived
    arrived = send(wave, lambda i: i ^ 8)
    token = piece(1, 0, 2048, across, None, wave)
    wave = wave + after(arrived, token)
    arrived = send(wave, lambda i: i ^ 2)
    token = piece(3, 0, 2048, passed, None, wave)
    wave = wave + after(arrived, token)
    arrived = send(wave, lambda i: i ^ 6)
    token = piece(2, 0, 2048, second, None, wave)
    return down(wave, arrived, constant, whole, pieces)


def solution(mesh):
    return jax.shard_map(
        body,
        mesh=mesh,
        in_specs=(
            P(None, "leaf"),
            P(None, "leaf"),
            P("leaf", None),
            P(None, "leaf", None),
            P("leaf", None),
        ),
        out_specs=P(None, "leaf"),
        check_vma=False,
    )
```
